512 devices in a mesh: ex: 128 (over y, z, core), pp: 4 (over x).
Axes of the slice: x: 4, y: 8, z: 8, core: 2. Of those that a mesh axis runs over, the one named last changes fastest.
Arguments:
- activations: bfloat16 [256, 128, 64, 128], P('ex', 'pp'), may hold values from -2 to 2
- output_grads: bfloat16 [256, 128, 32, 128], P('ex', 'pp'), may hold values from -2 to 2
- lengths: int32 [256], P('ex'), may hold values from 32 to 128
- whitening: bfloat16 [128, 4, 512, 2048], P('ex', 'pp'), may hold values from -0.125 to 0.125
Outputs:
- influence: float32 [128, 128], P('ex')
The draws below stay inside these ranges and needn't reach their ends.
Inputs may be any that keep to these rules, and one draw needn't show every extreme that they name: Positions from lengths[e] on are padding of example e.
All inputs are finite; a program needn't handle non-finite values.
Results may differ from the reference program's by a relative error of at most 0.0047.
Values may be sent and summed in bfloat16 or wider, within the bound.
A program may use at most 64 MiB of HBM per device.

```python
import math
import jax
import jax.numpy as jnp
from jax import lax

SEQ = 128
KIN = 64
KOUT = 32
ROWS = 512
ITERS = 3
FEAT = 2048
GROUP = 4
MOD_SEGMENT = 32
MODULES = 128
EXAMPLES = 256
QUERIES = 128
TRAIN = 128
N_EX = 128
N_PP = 4


def draw_activations(key, part):
    own_key = jax.random.fold_in(key, 11)
    single_key, common_key = jax.random.split(own_key)
    single = jnp.clip(jax.random.normal(single_key, (EXAMPLES, MODULES, KIN, SEQ), jnp.float32), -3.0, 3.0)
    common = jnp.clip(jax.random.normal(common_key, (MODULES, KIN, SEQ), jnp.float32), -3.0, 3.0)
    values = 0.3 * (0.6 * single + 0.8 * common[None])
    return jnp.clip(values, -2.0, 2.0).astype(jnp.bfloat16)


def draw_output_grads(key, part):
    own_key = jax.random.fold_in(key, 23)
    single_key, common_key, factor_key, pattern_key = jax.random.split(own_key, 4)
    rank_count = max(TRAIN // 16, 1)
    single = jnp.clip(jax.random.normal(single_key, (EXAMPLES, MODULES, KOUT, SEQ), jnp.float32), -3.0, 3.0)
    ramp_span = 3.0
    common = jnp.clip(jax.random.normal(common_key, (MODULES, KOUT, SEQ), jnp.float32), -3.0, 3.0)
    factors = jax.random.normal(factor_key, (EXAMPLES, rank_count), jnp.float32)
    pattern = jax.random.normal(pattern_key, (rank_count, MODULES), jnp.float32)
    mixing = jnp.dot(factors, pattern, precision=lax.Precision.HIGHEST) / math.sqrt(rank_count)
    example_index = lax.broadcasted_iota(jnp.int32, (EXAMPLES, MODULES), 0)
    is_train = example_index >= QUERIES
    mixing = jnp.where(is_train, jnp.clip(mixing, -2.0, 2.0), 0.0)
    position = example_index.astype(jnp.float32) / max(QUERIES - 1, 1)
    rising = jnp.where(is_train, 1.0, 1.0 + ramp_span * position)
    values = 0.3 * (0.6 * rising[:, :, None, None] * single + 0.8 * mixing[:, :, None, None] * common[None])
    return jnp.clip(values, -2.0, 2.0).astype(jnp.bfloat16)


def place_ends(entries, stream_key, smallest, high):
    longest = entries.shape.index(max(entries.shape))
    spots = []
    for shift in (0, 1):
        where = [jax.random.randint(jax.random.fold_in(stream_key, axis), (), 0, length) for axis, length in enumerate(entries.shape)]
        where[longest] = (where[longest] + shift) % entries.shape[longest]
        spots.append(tuple(where))
    return entries.at[spots[0]].set(smallest).at[spots[1]].set(high)


def steps_of(rng, dims, pieces, smallest, top_value):
    gain, own = 1.0, jax.random.fold_in(rng, 6)
    for axis_at, blocks in pieces:
        heights = jnp.exp(jax.random.uniform(jax.random.fold_in(own, axis_at), (blocks,), jnp.float32, smallest / len(pieces), top_value / len(pieces)))
        gain = gain * jnp.repeat(heights, dims[axis_at] // blocks).reshape([-1 if axis == axis_at else 1 for axis in range(len(dims))])
    return gain


def centred(key, shape, deviation, reach, cuts=(), held_as=jnp.bfloat16):
    loudness = steps_of(key, shape, cuts, -0.22, 0.18) if cuts else 1.0
    entries = jax.random.normal(key, shape, jnp.float32) * deviation * loudness
    return jnp.minimum(jnp.maximum(entries, -reach), reach).astype(held_as)


def setup_inputs(seed: int = 0) -> dict:
    streams_of = jax.random.split(jax.random.key(seed), 5)
    activations = draw_activations(jax.random.fold_in(streams_of[4], 71), 0)
    output_grads = draw_output_grads(jax.random.fold_in(streams_of[4], 71), 0)
    lengths = place_ends(jax.random.randint(streams_of[2], (EXAMPLES,), SEQ // 4, SEQ + 1), jax.random.fold_in(streams_of[2], 1), SEQ // 4, SEQ).astype(jnp.int32)
    whitening = centred(streams_of[3], (N_EX, N_PP, ROWS, FEAT), FEAT ** -0.5, 0.125, ((0, 128), (1, 4)))
    return dict(activations=activations, output_grads=output_grads, lengths=lengths, whitening=whitening)


def reference(activations, output_grads, lengths, whitening):
    token_mask = (lax.broadcasted_iota(jnp.int32, (EXAMPLES, SEQ), 1) < lengths[:, None]).astype(jnp.bfloat16)
    masked = output_grads * token_mask[:, None, None, :]
    stacked = whitening.reshape(MOD_SEGMENT, GROUP, N_PP, ROWS, FEAT)

    def module_terms(carry, module):
        cross_sum, gram_sum = carry
        segment = module // MOD_SEGMENT
        local = module % MOD_SEGMENT
        act_slice = lax.dynamic_index_in_dim(activations, module, 1, False).astype(jnp.float32)
        grad_slice = lax.dynamic_index_in_dim(masked, module, 1, False).astype(jnp.float32)
        gradient = jnp.einsum('ekt,ejt->ekj', grad_slice, act_slice).reshape(EXAMPLES, FEAT).astype(jnp.bfloat16)
        matrix = lax.dynamic_index_in_dim(lax.dynamic_index_in_dim(stacked, local, 0, False), segment, 1, False)
        matrix = matrix.reshape(FEAT, FEAT)
        whitened = lax.dot_general(gradient, matrix, (((1,), (1,)), ((), ())), preferred_element_type=jnp.float32).astype(jnp.bfloat16)
        query_part = whitened[:QUERIES]
        train_part = whitened[QUERIES:]
        cross_sum = cross_sum + lax.dot_general(query_part, train_part, (((1,), (1,)), ((), ())), preferred_element_type=jnp.float32)
        gram_sum = gram_sum + lax.dot_general(train_part, train_part, (((1,), (1,)), ((), ())), preferred_element_type=jnp.float32)
        return ((cross_sum, gram_sum), None)
    start = (jnp.zeros((QUERIES, TRAIN), jnp.float32), jnp.zeros((TRAIN, TRAIN), jnp.float32))
    (cross_sum, gram_sum), _ = lax.scan(module_terms, start, jnp.arange(MODULES, dtype=jnp.int32))
    count_all = MODULES * FEAT
    scores = cross_sum / math.sqrt(count_all)
    kernel = gram_sum / count_all
    clip_level = 0.06 * math.sqrt(QUERIES * TRAIN)
    answer = jnp.zeros((QUERIES, TRAIN), jnp.float32)
    for iteration in range(ITERS):
        residual = scores - jnp.dot(answer, kernel, precision=lax.Precision.HIGHEST) - 0.5 * answer
        magnitude = jnp.sqrt(jnp.sum(residual * residual) + 1e-06)
        answer = answer + jnp.minimum(0.5, clip_level / magnitude) * residual
    return answer
```

```python
import functools
import math

import jax
import jax.numpy as jnp
from jax import lax
from jax.experimental import pallas as pl
from jax.experimental.pallas import tpu as pltpu
from jax.sharding import PartitionSpec as P

MESH = pl.DeviceIdType.MESH
BF = jnp.bfloat16
F32 = jnp.float32
NY, NZ, NC, NX = 8, 8, 2, 4
NT = (((1,), (1,)), ((), ()))

step_rate = 0.5
ridge_shift = 0.5
clip_frac = 0.06


def total(value):
    return jnp.sum(jnp.sum(value, axis=1, keepdims=True), axis=0, keepdims=True)


def kernel(
    len_ref, act_hbm, grad_hbm, w_hbm, out_ref,
    act, grad, w_in, w, gbuf, near_buf, feat, white, part, rs_z, rs_y, rs_x, mine, full, answer,
    in_sem, w_sem, p1_send, p1_recv, p2_send, p2_recv, rs_send, rs_recv,
):
    ex = lax.axis_index("ex")
    x = lax.axis_index("pp")
    y = ex // (NZ * NC)
    z = (ex // NC) % NZ
    c = ex % NC
    half = y // 4
    odd = z % 2
    mate_z = z + 1 - 2 * odd

    def at(y_, z_, c_, x_=None):
        return ((y_ * NZ + z_) * NC + c_, x if x_ is None else x_)

    def row_of(i):
        return (half + i // 4) % 2 * 4 + (y + i) % 4

    def load(i):
        rows = pl.ds(row_of(i) * 4, 4)
        return (
            pltpu.make_async_copy(act_hbm.at[:, rows], act.at[:, rows], in_sem.at[0, i]),
            pltpu.make_async_copy(grad_hbm.at[:, rows], grad.at[:, rows], in_sem.at[1, i]),
        )

    for i in range(NY):
        for copy in load(i):
            copy.start()
    w_copy = pltpu.make_async_copy(w_hbm.at[0, 0], w_in, w_sem)
    w_copy.start()

    barrier = pltpu.get_barrier_semaphore()
    toward = 2 * odd - 1

    def greet(i, _):
        y_, d = i // 4, i % 4

        @pl.when(jnp.logical_not(jnp.logical_and(y_ == y, d == 0)))
        def _():
            z_ = (z + toward * d + NZ) % NZ
            pl.semaphore_signal(barrier, inc=1, device_id=at(y_, z_, c), device_id_type=MESH)

        return 0

    lax.fori_loop(0, 32, greet, 0)
    for i in range(1, 16):
        j = (z * NC + c + i) % 16
        pl.semaphore_signal(barrier, inc=1, device_id=at(y, j // NC, j % NC), device_id_type=MESH)
    for i in range(1, NX):
        pl.semaphore_signal(barrier, inc=1, device_id=at(y, z, c, (x + i) % NX), device_id_type=MESH)

    lane_low = lax.broadcasted_iota(jnp.int32, (16, 128), 1) < 64
    spots = lax.broadcasted_iota(jnp.int32, (1, 128), 1)
    masks = [(spots < len_ref[e]).astype(F32).astype(BF) for e in range(2)]

    s_own = ((z + 1) // 2) % 4
    zl = (z + 1) % 2
    slot = (y % 4) * 2 + zl

    def target(p):
        d = (2 * p - z + NZ) % NZ
        chip = jnp.where(d < 4, 2 * p, 2 * p + 1)
        far = jnp.where(d < 4, d // 2, (7 - d) // 2)
        return chip, far

    def gradients(i):
        y_ = row_of(i)
        for copy in load(i):
            copy.wait()
        for k in range(4):
            m = y_ * 4 + k
            for e in range(2):
                a = act[e, m]
                g = grad[e, m] * masks[e]
                twice = jnp.concatenate([a, a], axis=0)
                both = lax.dot_general(g, twice, NT, preferred_element_type=F32)
                gbuf[m, e] = jnp.where(lane_low, both[:16], both[16:]).astype(BF)

    def send(i, _):
        y_ = row_of(i)
        for p in range(4):
            m = y_ * 4 + p
            chip, far = target(p)
            here = jnp.logical_and(y_ == y, chip == z)

            @pl.when(here)
            def _():
                pltpu.make_async_copy(
                    gbuf.at[m], near_buf.at[half, far, slot], p1_recv.at[half, far]
                ).start()

            @pl.when(jnp.logical_not(here))
            def _():
                pltpu.make_async_remote_copy(
                    src_ref=gbuf.at[m],
                    dst_ref=near_buf.at[half, far, slot],
                    send_sem=p1_send,
                    recv_sem=p1_recv.at[half, far],
                    device_id=at(y_, chip, c),
                    device_id_type=MESH,
                ).start()

    gradients(0)
    pl.semaphore_wait(barrier, 31 + 15 + 3)
    send(0, 0)

    def produce(i, _):
        gradients(i)
        send(i, 0)
        return 0

    lax.fori_loop(1, NY, produce, 0)

    w_copy.wait()

    def reorder(r, _):
        rows = pl.ds(r * 32, 32)
        low = lax.broadcasted_iota(jnp.int32, (32, 128), 1) < 64
        for a in range(8):
            t = w_in[rows, a * 128:(a + 1) * 128]
            u = w_in[rows, (8 + a) * 128:(9 + a) * 128]
            t_turned = jnp.concatenate([t[:, 64:], t[:, :64]], axis=1)
            u_turned = jnp.concatenate([u[:, 64:], u[:, :64]], axis=1)
            w[rows, 2 * a * 128:(2 * a + 1) * 128] = jnp.where(low, t, u_turned)
            w[rows, (2 * a + 1) * 128:(2 * a + 2) * 128] = jnp.where(low, t_turned, u)
        return 0

    lax.fori_loop(0, 16, reorder, 0)

    to = lax.broadcasted_iota(jnp.int32, (256, 256), 0)
    frm = lax.broadcasted_iota(jnp.int32, (256, 256), 1)
    shuffle = (frm == (to % 16) * 16 + to // 16).astype(F32).astype(BF)

    def block_rows(q, z_, c_):
        h = (half + q // 2) % 2
        p = z_ // 2
        s = jnp.where(z_ % 2 == 0, p - q % 2 + 4, p + 1 + q % 2) % 4
        return pl.ds(pl.multiple_of(h * 128 + s * 32 + c_ * 16, 16), 16)

    def pair_copy(kind, q):
        rows = block_rows(q, mate_z if kind == 2 else z, c)
        return pltpu.make_async_remote_copy(
            src_ref=feat.at[rows],
            dst_ref=feat.at[rows],
            send_sem=p2_send.at[kind, q],
            recv_sem=p2_recv.at[kind, q],
            device_id=at(y, mate_z, c) if kind == 0 else at(y, z, 1 - c),
            device_id_type=MESH,
        )

    def arrived(kind, q):
        rows = block_rows(q, z if kind == 1 else mate_z, c if kind == 0 else 1 - c)
        pltpu.make_async_copy(feat.at[rows], feat.at[rows], p2_recv.at[kind, q]).wait()

    def whiten(h):
        rows = pl.ds(pl.multiple_of(h * 128, 128), 128)
        white[rows] = lax.dot_general(feat[rows], w[...], NT, preferred_element_type=F32).astype(BF)

    for q in range(4):
        h = (half + q // 2) % 2
        block = near_buf.at[h, q % 2]
        pltpu.make_async_copy(block, block, p1_recv.at[h, q % 2]).wait()
        tiles = near_buf[h, q % 2].reshape(256, 128)
        turned = jnp.dot(shuffle, tiles, preferred_element_type=F32).astype(BF)
        rows = block_rows(q, z, c)
        for kk in range(16):
            feat[rows, kk * 128:(kk + 1) * 128] = turned[kk * 16:(kk + 1) * 16]
        pair_copy(0, q).start()
        pair_copy(1, q).start()
        if q > 0:
            arrived(0, q - 1)
            pair_copy(2, q - 1).start()
    for q in range(2):
        arrived(1, q)
        arrived(2, q)
    whiten(half)
    arrived(0, 3)
    pair_copy(2, 3).start()
    for q in range(2, 4):
        arrived(1, q)
        arrived(2, q)
    whiten((half + 1) % 2)

    part[...] = lax.dot_general(white[...], white[128:], NT, preferred_element_type=F32)

    me16 = z * NC + c
    for i in range(1, 16):
        j = (me16 + i) % 16
        pltpu.make_async_remote_copy(
            src_ref=part.at[pl.ds(pl.multiple_of(j * 16, 16), 16)],
            dst_ref=rs_z.at[15 - i],
            send_sem=rs_send.at[0],
            recv_sem=rs_recv.at[0],
            device_id=at(y, j // NC, j % NC),
            device_id_type=MESH,
        ).start()
    own = part[pl.ds(pl.multiple_of(me16 * 16, 16), 16)]
    pltpu.make_async_copy(rs_z, rs_z, rs_recv.at[0]).wait()
    mine[0] = own + jnp.sum(rs_z[...], axis=0)

    for i in range(1, NY):
        pltpu.make_async_remote_copy(
            src_ref=mine.at[0],
            dst_ref=rs_y.at[y],
            send_sem=rs_send.at[1],
            recv_sem=rs_recv.at[1],
            device_id=at((y + i) % NY, z, c),
            device_id_type=MESH,
        ).start()
    rs_y[y] = mine[0]
    pltpu.make_async_copy(rs_y.at[1:], rs_y.at[1:], rs_recv.at[1]).wait()
    mine[1] = jnp.sum(rs_y[...], axis=0)

    for i in range(1, NX):
        pltpu.make_async_remote_copy(
            src_ref=mine.at[1],
            dst_ref=rs_x.at[x],
            send_sem=rs_send.at[2],
            recv_sem=rs_recv.at[2],
            device_id=at(y, z, c, (x + i) % NX),
            device_id_type=MESH,
        ).start()
    rs_x[x] = mine[1]
    pltpu.make_async_copy(rs_x.at[1:], rs_x.at[1:], rs_recv.at[2]).wait()
    my_rows = pl.ds(pl.multiple_of(me16 * 16, 16), 16)
    full[my_rows] = jnp.sum(rs_x[...], axis=0)

    for i in range(1, 16):
        j = (me16 + i) % 16
        pltpu.make_async_remote_copy(
            src_ref=full.at[my_rows],
            dst_ref=full.at[my_rows],
            send_sem=rs_send.at[3],
            recv_sem=rs_recv.at[3],
            device_id=at(y, j // NC, j % NC),
            device_id_type=MESH,
        ).start()
    pltpu.make_async_copy(full.at[:240], full.at[:240], rs_recv.at[3]).wait()

    count = 32 * NX * 2048
    scores = full[:128] * (1.0 / math.sqrt(count))
    gram = full[128:] * (1.0 / count)
    level = clip_frac * math.sqrt(128 * 128)
    exact = functools.partial(jnp.dot, precision=lax.Precision.HIGHEST, preferred_element_type=F32)

    def pace(residual):
        return jnp.minimum(step_rate, level * lax.rsqrt(total(residual * residual) + 1e-06))

    now = pace(scores) * scores
    for _ in range(2):
        residual = scores - exact(now, gram) - ridge_shift * now
        now = now + pace(residual) * residual
    answer[...] = now

    q_y, q_z, q_c, q_e = ex // 32, (ex // 4) % 8, (ex // 2) % 2, ex % 2
    row = ((q_z + 1) // 2) % 4 * 32 + q_c * 16 + q_y * 4 + (q_z + 1) % 2 * 2 + q_e
    line = jnp.broadcast_to(answer[pl.ds(row, 1)], (8, 128))
    t = lax.broadcasted_iota(jnp.int32, (128, 128), 1)
    t_z = (t // 4) % 8
    spot = ((t_z + 1) // 2) % 4 * 32 + (t // 2) % 2 * 16 + t // 32 * 4 + (t_z + 1) % 2 * 2 + t % 2
    pick = (lax.broadcasted_iota(jnp.int32, (128, 128), 0) == spot).astype(F32)
    out_ref[...] = exact(line, pick)[:1]

    pltpu.make_async_copy(gbuf.at[:31], gbuf.at[:31], p1_send).wait()
    for kind in range(3):
        for q in range(4):
            pair_copy(kind, q).wait_send()
    pltpu.make_async_copy(rs_z, rs_z, rs_send.at[0]).wait()
    pltpu.make_async_copy(rs_y.at[1:], rs_y.at[1:], rs_send.at[1]).wait()
    pltpu.make_async_copy(rs_x.at[1:], rs_x.at[1:], rs_send.at[2]).wait()
    pltpu.make_async_copy(full.at[:240], full.at[:240], rs_send.at[3]).wait()


def body(activations, output_grads, lengths, whitening):
    hbm = pl.BlockSpec(memory_space=pl.ANY)
    return pl.pallas_call(
        kernel,
        out_shape=jax.ShapeDtypeStruct((1, 128), F32),
        in_specs=[pl.BlockSpec(memory_space=pltpu.SMEM), hbm, hbm, hbm],
        out_specs=pl.BlockSpec(memory_space=pltpu.VMEM),
        scratch_shapes=[
            pltpu.VMEM((2, 32, 64, 128), BF),
            pltpu.VMEM((2, 32, 32, 128), BF),
            pltpu.VMEM((512, 2048), BF),
            pltpu.VMEM((512, 2048), BF),
            pltpu.VMEM((32, 2, 16, 128), BF),
            pltpu.VMEM((2, 2, 8, 2, 16, 128), BF),
            pltpu.VMEM((256, 2048), BF),
            pltpu.VMEM((256, 512), BF),
            pltpu.VMEM((256, 128), F32),
            pltpu.VMEM((15, 16, 128), F32),
            pltpu.VMEM((8, 16, 128), F32),
            pltpu.VMEM((4, 16, 128), F32),
            pltpu.VMEM((2, 16, 128), F32),
            pltpu.VMEM((256, 128), F32),
            pltpu.VMEM((128, 128), F32),
            pltpu.SemaphoreType.DMA((2, 8)),
            pltpu.SemaphoreType.DMA,
            pltpu.SemaphoreType.DMA,
            pltpu.SemaphoreType.DMA((2, 2)),
            pltpu.SemaphoreType.DMA((3, 4)),
            pltpu.SemaphoreType.DMA((3, 4)),
            pltpu.SemaphoreType.DMA((4,)),
            pltpu.SemaphoreType.DMA((4,)),
        ],
        compiler_params=pltpu.CompilerParams(
            collective_id=0, has_side_effects=True, vmem_limit_bytes=40 * 1024 * 1024
        ),
        cost_estimate=pl.CostEstimate(flops=700_000_000, bytes_accessed=4_000_000, transcendentals=0),
    )(lengths, activations, output_grads, whitening)


def solution(mesh):
    placed = (P("ex", "pp", None, None), P("ex", "pp", None, None), P("ex"), P("ex", "pp", None, None))

    def program(activations, output_grads, lengths, whitening):
        return jax.shard_map(body, mesh=mesh, in_specs=placed, out_specs=P("ex", None), check_vma=False)(
            activations, output_grads, lengths, whitening
        )

    return program
```

```python
import functools
import math

import jax
import jax.numpy as jnp
from jax import lax
from jax.experimental import pallas as pl
from jax.experimental.pallas import tpu as pltpu
from jax.sharding import PartitionSpec as P

MESH = pl.DeviceIdType.MESH
BF = jnp.bfloat16
F32 = jnp.float32
NY, NZ, NC, NX = 8, 8, 2, 4
NT = (((1,), (1,)), ((), ()))

step_rate = 0.5
ridge_shift = 0.5
clip_frac = 0.06


def total(value):
    return jnp.sum(jnp.sum(value, axis=1, keepdims=True), axis=0, keepdims=True)


def kernel(
    len_hbm, act_hbm, grad_hbm, w_hbm, out_ref,
    len_ref,     act, grad, w_in, w, gbuf, near_buf, shuffle, feat, white, part, rs_z, rs_y, rs_x, mine, full, answer,
    len_sem, in_sem, w_sem, p1_send, p1_recv, p2_send, p2_recv, rs_send, rs_recv,
):
    ex = lax.axis_index("ex")
    x = lax.axis_index("pp")
    y = ex // (NZ * NC)
    z = (ex // NC) % NZ
    c = ex % NC
    half = y // 4
    odd = z % 2
    mate_z = z + 1 - 2 * odd

    def at(y_, z_, c_, x_=None):
        return ((y_ * NZ + z_) * NC + c_, x if x_ is None else x_)

    barrier = pltpu.get_barrier_semaphore()
    toward = 2 * odd - 1

    def greet(device):
        pl.semaphore_signal(barrier, inc=1, device_id=device, device_id_type=MESH)

    for dy in (4, 3, 5, 2, 6, 1, 7, 0):
        for d in (3, 2, 1, 0):
            if dy or d:
                greet(at((y + dy) % NY, (z + toward * d + NZ) % NZ, c))
    for i in (8, 9, 7, 6, 10, 11, 5, 4, 12, 13, 3, 2, 14, 15, 1):
        j = (z * NC + c + i) % 16
        greet(at(y, j // NC, j % NC))
    for i in (2, 1, 3):
        greet(at(y, z, c, (x + i) % NX))

    len_copy = pltpu.make_async_copy(len_hbm, len_ref, len_sem)

    def load(j):
        rows = pl.ds(j * 8, 8)
        return (
            pltpu.make_async_copy(act_hbm.at[:, rows], act.at[:, rows], in_sem.at[0, j]),
            pltpu.make_async_copy(grad_hbm.at[:, rows], grad.at[:, rows], in_sem.at[1, j]),
        )

    len_copy.start()
    for j in range(4):
        for copy in load(j):
            copy.start()
    w_copy = pltpu.make_async_copy(w_hbm.at[0, 0], w_in, w_sem)
    w_copy.start()

    lane_low = lax.broadcasted_iota(jnp.int32, (16, 128), 1) < 64
    spots = lax.broadcasted_iota(jnp.int32, (1, 128), 1)
    len_copy.wait()
    masks = [(spots < len_ref[e]).astype(F32).astype(BF) for e in range(2)]

    def gradients(j, _):
        for copy in load(j):
            copy.wait()
        for k in range(8):
            m = j * 8 + k
            for e in range(2):
                a = act[e, m]
                g = grad[e, m] * masks[e]
                twice = jnp.concatenate([a, a], axis=0)
                both = lax.dot_general(g, twice, NT, preferred_element_type=F32)
                gbuf[m, e] = jnp.where(lane_low, both[:16], both[16:]).astype(BF)
        return 0

    lax.fori_loop(0, 4, gradients, 0)

    slot = (y % 4) * 2 + (z + 1) % 2

    def send(group, _):
        far = group % 2
        for k in range(2):
            p = (z // 2 + toward * (2 * far + k) + 4) % 4
            chip = jnp.where((2 * p - z + NZ) % NZ < 4, 2 * p, 2 * p + 1)
            for i in range(4):
                y_ = (half + group // 2) % 2 * 4 + (y + i) % 4
                m = y_ * 4 + p
                here = jnp.logical_and(y_ == y, chip == z)

                def remote():
                    pltpu.make_async_remote_copy(
                        src_ref=gbuf.at[m],
                        dst_ref=near_buf.at[half, far, slot],
                        send_sem=p1_send,
                        recv_sem=p1_recv.at[half, far],
                        device_id=at(y_, chip, c),
                        device_id_type=MESH,
                    ).start()

                if k == 0 and i == 0:

                    @pl.when(here)
                    def _():
                        pltpu.make_async_copy(
                            gbuf.at[m], near_buf.at[half, far, slot], p1_recv.at[half, far]
                        ).start()

                    pl.when(jnp.logical_not(here))(remote)
                else:
                    remote()
        return 0

    pl.semaphore_wait(barrier, 31 + 15 + 3)
    lax.fori_loop(0, 4, send, 0)

    w_copy.wait()

    def reorder(r, _):
        rows = pl.ds(r * 32, 32)
        low = lax.broadcasted_iota(jnp.int32, (32, 128), 1) < 64
        for a in range(8):
            t = w_in[rows, a * 128:(a + 1) * 128]
            u = w_in[rows, (8 + a) * 128:(9 + a) * 128]
            t_turned = jnp.concatenate([t[:, 64:], t[:, :64]], axis=1)
            u_turned = jnp.concatenate([u[:, 64:], u[:, :64]], axis=1)
            w[rows, 2 * a * 128:(2 * a + 1) * 128] = jnp.where(low, t, u_turned)
            w[rows, (2 * a + 1) * 128:(2 * a + 2) * 128] = jnp.where(low, t_turned, u)
        return 0

    lax.fori_loop(0, 16, reorder, 0)

    to = lax.broadcasted_iota(jnp.int32, (256, 256), 0)
    frm = lax.broadcasted_iota(jnp.int32, (256, 256), 1)
    shuffle[...] = (frm == (to % 16) * 16 + to // 16).astype(F32).astype(BF)

    def block_rows(q, z_, c_):
        h = (half + q // 2) % 2
        p = z_ // 2
        s = jnp.where(z_ % 2 == 0, p - q % 2 + 4, p + 1 + q % 2) % 4
        return pl.ds(pl.multiple_of(h * 128 + s * 32 + c_ * 16, 16), 16)

    def pair_copy(kind, q):
        rows = block_rows(q, mate_z if kind == 2 else z, c)
        return pltpu.make_async_remote_copy(
            src_ref=feat.at[rows],
            dst_ref=feat.at[rows],
            send_sem=p2_send.at[kind, q],
            recv_sem=p2_recv.at[kind, q],
            device_id=at(y, mate_z, c) if kind == 0 else at(y, z, 1 - c),
            device_id_type=MESH,
        )

    def arrived(kind, q):
        rows = block_rows(q, z if kind == 1 else mate_z, c if kind == 0 else 1 - c)
        pltpu.make_async_copy(feat.at[rows], feat.at[rows], p2_recv.at[kind, q]).wait()

    def whiten(h):
        rows = pl.ds(pl.multiple_of(h * 128, 128), 128)
        white[rows] = lax.dot_general(feat[rows], w[...], NT, preferred_element_type=F32).astype(BF)

    for q in range(4):
        h = (half + q // 2) % 2
        block = near_buf.at[h, q % 2]
        pltpu.make_async_copy(block, block, p1_recv.at[h, q % 2]).wait()
        tiles = near_buf[h, q % 2].reshape(256, 128)
        turned = jnp.dot(shuffle[...], tiles, preferred_element_type=F32).astype(BF)
        rows = block_rows(q, z, c)
        for kk in range(16):
            feat[rows, kk * 128:(kk + 1) * 128] = turned[kk * 16:(kk + 1) * 16]
        pair_copy(0, q).start()
        pair_copy(1, q).start()
        if q > 0:
            arrived(0, q - 1)
            pair_copy(2, q - 1).start()
    for q in range(2):
        arrived(1, q)
        arrived(2, q)
    whiten(half)
    arrived(0, 3)
    pair_copy(2, 3).start()
    for q in range(2, 4):
        arrived(1, q)
        arrived(2, q)
    whiten((half + 1) % 2)

    part[...] = lax.dot_general(white[...], white[128:], NT, preferred_element_type=F32).astype(BF)

    me16 = z * NC + c
    for i in range(1, 16):
        j = (me16 + i) % 16
        pltpu.make_async_remote_copy(
            src_ref=part.at[pl.ds(pl.multiple_of(j * 16, 16), 16)],
            dst_ref=rs_z.at[15 - i],
            send_sem=rs_send.at[0],
            recv_sem=rs_recv.at[0],
            device_id=at(y, j // NC, j % NC),
            device_id_type=MESH,
        ).start()
    own = part[pl.ds(pl.multiple_of(me16 * 16, 16), 16)].astype(F32)
    pltpu.make_async_copy(rs_z, rs_z, rs_recv.at[0]).wait()
    mine[0] = (own + jnp.sum(rs_z[...].astype(F32), axis=0)).astype(BF)

    for i in range(1, NY):
        pltpu.make_async_remote_copy(
            src_ref=mine.at[0],
            dst_ref=rs_y.at[y],
            send_sem=rs_send.at[1],
            recv_sem=rs_recv.at[1],
            device_id=at((y + i) % NY, z, c),
            device_id_type=MESH,
        ).start()
    rs_y[y] = mine[0]
    pltpu.make_async_copy(rs_y.at[1:], rs_y.at[1:], rs_recv.at[1]).wait()
    mine[1] = jnp.sum(rs_y[...].astype(F32), axis=0).astype(BF)

    for i in range(1, NX):
        pltpu.make_async_remote_copy(
            src_ref=mine.at[1],
            dst_ref=rs_x.at[x],
            send_sem=rs_send.at[2],
            recv_sem=rs_recv.at[2],
            device_id=at(y, z, c, (x + i) % NX),
            device_id_type=MESH,
        ).start()
    rs_x[x] = mine[1]
    pltpu.make_async_copy(rs_x.at[1:], rs_x.at[1:], rs_recv.at[2]).wait()
    my_rows = pl.ds(pl.multiple_of(me16 * 16, 16), 16)
    full[my_rows] = jnp.sum(rs_x[...].astype(F32), axis=0).astype(BF)

    for i in range(1, 16):
        j = (me16 + i) % 16
        pltpu.make_async_remote_copy(
            src_ref=full.at[my_rows],
            dst_ref=full.at[my_rows],
            send_sem=rs_send.at[3],
            recv_sem=rs_recv.at[3],
            device_id=at(y, j // NC, j % NC),
            device_id_type=MESH,
        ).start()
    pltpu.make_async_copy(full.at[:240], full.at[:240], rs_recv.at[3]).wait()

    count = 32 * NX * 2048
    scores16 = full[:128] * BF(1.0 / math.sqrt(count))
    gram = full[128:] * BF(1.0 / count)
    scores = scores16.astype(F32)
    level = clip_frac * math.sqrt(128 * 128)

    def times_gram(value):
        high = value.astype(BF)
        rest = value - high.astype(F32)
        middle = rest.astype(BF)
        low = (rest - middle.astype(F32)).astype(BF)
        product = jnp.dot(jnp.concatenate([high, middle, low], axis=0), gram, preferred_element_type=F32)
        return product[:128] + product[128:256] + product[256:]

    def pace(residual):
        return jnp.minimum(step_rate, level * lax.rsqrt(total(residual * residual) + 1e-06))

    scores_gram = jnp.dot(scores16, gram, preferred_element_type=F32)
    scores_gram2 = times_gram(scores_gram)
    first = pace(scores)
    now, now_gram = first * scores, first * scores_gram
    residual = scores - now_gram - ridge_shift * now
    residual_gram = scores_gram - first * scores_gram2 - ridge_shift * now_gram
    second = pace(residual)
    now, now_gram = now + second * residual, now_gram + second * residual_gram
    residual = scores - now_gram - ridge_shift * now
    now = now + pace(residual) * residual
    answer[...] = now

    q_y, q_z, q_c, q_e = ex // 32, (ex // 4) % 8, (ex // 2) % 2, ex % 2
    row = ((q_z + 1) // 2) % 4 * 32 + q_c * 16 + q_y * 4 + (q_z + 1) % 2 * 2 + q_e
    line = jnp.broadcast_to(answer[pl.ds(row, 1)], (8, 128))
    t = lax.broadcasted_iota(jnp.int32, (128, 128), 1)
    t_z = (t // 4) % 8
    spot = ((t_z + 1) // 2) % 4 * 32 + (t // 2) % 2 * 16 + t // 32 * 4 + (t_z + 1) % 2 * 2 + t % 2
    pick = (lax.broadcasted_iota(jnp.int32, (128, 128), 0) == spot).astype(F32)
    out_ref[...] = jnp.dot(line, pick, precision=lax.Precision.HIGHEST, preferred_element_type=F32)[:1]

    pltpu.make_async_copy(gbuf.at[:31], gbuf.at[:31], p1_send).wait()
    for kind in range(3):
        for q in range(4):
            pair_copy(kind, q).wait_send()
    pltpu.make_async_copy(rs_z, rs_z, rs_send.at[0]).wait()
    pltpu.make_async_copy(rs_y.at[1:], rs_y.at[1:], rs_send.at[1]).wait()
    pltpu.make_async_copy(rs_x.at[1:], rs_x.at[1:], rs_send.at[2]).wait()
    pltpu.make_async_copy(full.at[:240], full.at[:240], rs_send.at[3]).wait()


def body(activations, output_grads, lengths, whitening):
    hbm = pl.BlockSpec(memory_space=pltpu.HBM)
    return pl.pallas_call(
        kernel,
        out_shape=jax.ShapeDtypeStruct((1, 128), F32),
        in_specs=[hbm, hbm, hbm, hbm],
        out_specs=pl.BlockSpec(memory_space=pltpu.VMEM),
        scratch_shapes=[
            pltpu.SMEM((2,), jnp.int32),
            pltpu.VMEM((2, 32, 64, 128), BF),
            pltpu.VMEM((2, 32, 32, 128), BF),
            pltpu.VMEM((512, 2048), BF),
            pltpu.VMEM((512, 2048), BF),
            pltpu.VMEM((32, 2, 16, 128), BF),
            pltpu.VMEM((2, 2, 8, 2, 16, 128), BF),
            pltpu.VMEM((256, 256), BF),
            pltpu.VMEM((256, 2048), BF),
            pltpu.VMEM((256, 512), BF),
            pltpu.VMEM((256, 128), BF),
            pltpu.VMEM((15, 16, 128), BF),
            pltpu.VMEM((8, 16, 128), BF),
            pltpu.VMEM((4, 16, 128), BF),
            pltpu.VMEM((2, 16, 128), BF),
            pltpu.VMEM((256, 128), BF),
            pltpu.VMEM((128, 128), F32),
            pltpu.SemaphoreType.DMA,
            pltpu.SemaphoreType.DMA((2, 4)),
            pltpu.SemaphoreType.DMA,
            pltpu.SemaphoreType.DMA,
            pltpu.SemaphoreType.DMA((2, 2)),
            pltpu.SemaphoreType.DMA((3, 4)),
            pltpu.SemaphoreType.DMA((3, 4)),
            pltpu.SemaphoreType.DMA((4,)),
            pltpu.SemaphoreType.DMA((4,)),
        ],
        compiler_params=pltpu.CompilerParams(
            collective_id=0, has_side_effects=True, vmem_limit_bytes=62 * 1024 * 1024
        ),
        cost_estimate=pl.CostEstimate(flops=700_000_000, bytes_accessed=4_000_000, transcendentals=0),
    )(lengths, activations, output_grads, whitening)


def solution(mesh):
    placed = (P("ex", "pp", None, None), P("ex", "pp", None, None), P("ex"), P("ex", "pp", None, None))

    def program(activations, output_grads, lengths, whitening):
        return jax.shard_map(body, mesh=mesh, in_specs=placed, out_specs=P("ex", None), check_vma=False)(
            activations, output_grads, lengths, whitening
        )

    return program
```

```python
import functools
import math

import jax
import jax.numpy as jnp
from jax import lax
from jax.experimental import pallas as pl
from jax.experimental.pallas import tpu as pltpu
from jax.sharding import PartitionSpec as P

MESH = pl.DeviceIdType.MESH
BF = jnp.bfloat16
F32 = jnp.float32
NY, NZ, NC, NX = 8, 8, 2, 4
NT = (((1,), (1,)), ((), ()))

step_rate = 0.5
ridge_shift = 0.5
clip_frac = 0.06


def total(value):
    return jnp.sum(jnp.sum(value, axis=1, keepdims=True), axis=0, keepdims=True)


def kernel(
    len_hbm, act_hbm, grad_hbm, w_hbm, out_ref,
    len_ref,     act, grad, w_in, w, gbuf, near_buf, shuffle, feat, white, part, rs_a, rs_z, rs_y, mine, full, answer,
    len_sem, in_sem, w_sem, p1_send, p1_recv, p2_send, p2_recv, rs_send, rs_recv,
):
    ex = lax.axis_index("ex")
    x = lax.axis_index("pp")
    y = ex // (NZ * NC)
    z = (ex // NC) % NZ
    c = ex % NC
    half = y // 4
    odd = z % 2
    mate_z = z + 1 - 2 * odd

    def at(y_, z_, c_, x_=None):
        return ((y_ * NZ + z_) * NC + c_, x if x_ is None else x_)

    barrier = pltpu.get_barrier_semaphore()
    toward = 2 * odd - 1

    def greet(device):
        pl.semaphore_signal(barrier, inc=1, device_id=device, device_id_type=MESH)

    for dy in (4, 3, 5, 2, 6, 1, 7, 0):
        for d in (3, 2, 1, 0):
            if dy or d:
                greet(at((y + dy) % NY, (z + toward * d + NZ) % NZ, c))
    for i in (4, 3, 5, 2, 6, 1, 7):
        greet(at(y, (z + i) % NZ, c))
    for i in (4, 5, 2, 3, 6, 7, 1):
        greet(at(y, z, (c + i) % 2, (x + i // 2) % NX))

    len_copy = pltpu.make_async_copy(len_hbm, len_ref, len_sem)

    def load(j):
        rows = pl.ds(j * 8, 8)
        return (
            pltpu.make_async_copy(act_hbm.at[:, rows], act.at[:, rows], in_sem.at[0, j]),
            pltpu.make_async_copy(grad_hbm.at[:, rows], grad.at[:, rows], in_sem.at[1, j]),
        )

    len_copy.start()
    for j in range(4):
        for copy in load(j):
            copy.start()
    w_copy = pltpu.make_async_copy(w_hbm.at[0, 0], w_in, w_sem)
    w_copy.start()

    lane_low = lax.broadcasted_iota(jnp.int32, (16, 128), 1) < 64
    spots = lax.broadcasted_iota(jnp.int32, (1, 128), 1)
    len_copy.wait()
    masks = [(spots < len_ref[e]).astype(F32).astype(BF) for e in range(2)]

    def gradients(j, _):
        for copy in load(j):
            copy.wait()
        for k in range(8):
            m = j * 8 + k
            for e in range(2):
                a = act[e, m]
                g = grad[e, m] * masks[e]
                twice = jnp.concatenate([a, a], axis=0)
                both = lax.dot_general(g, twice, NT, preferred_element_type=F32)
                gbuf[m, e] = jnp.where(lane_low, both[:16], both[16:]).astype(BF)
        return 0

    lax.fori_loop(0, 4, gradients, 0)

    slot = (y % 4) * 2 + (z + 1) % 2
    pl.semaphore_wait(barrier, 31 + 7 + 7)
    for far in range(2):
        for dy in (4, 3, 5, 2, 6, 1, 7, 0):
            y_ = (y + dy) % NY
            for k in range(2):
                p = (z // 2 + toward * (2 * far + k) + 4) % 4
                chip = jnp.where((2 * p - z + NZ) % NZ < 4, 2 * p, 2 * p + 1)
                source, target = gbuf.at[y_ * 4 + p], near_buf.at[half, far, slot]
                if dy == 0 and far == 0 and k == 0:
                    pltpu.make_async_copy(source, target, p1_recv.at[half, far]).start()
                else:
                    pltpu.make_async_remote_copy(
                        src_ref=source,
                        dst_ref=target,
                        send_sem=p1_send,
                        recv_sem=p1_recv.at[half, far],
                        device_id=at(y_, chip, c),
                        device_id_type=MESH,
                    ).start()

    w_copy.wait()

    def reorder(r, _):
        rows = pl.ds(r * 32, 32)
        low = lax.broadcasted_iota(jnp.int32, (32, 128), 1) < 64
        for a in range(8):
            t = w_in[rows, a * 128:(a + 1) * 128]
            u = w_in[rows, (8 + a) * 128:(9 + a) * 128]
            t_turned = jnp.concatenate([t[:, 64:], t[:, :64]], axis=1)
            u_turned = jnp.concatenate([u[:, 64:], u[:, :64]], axis=1)
            w[rows, 2 * a * 128:(2 * a + 1) * 128] = jnp.where(low, t, u_turned)
            w[rows, (2 * a + 1) * 128:(2 * a + 2) * 128] = jnp.where(low, t_turned, u)
        return 0

    lax.fori_loop(0, 16, reorder, 0)

    to = lax.broadcasted_iota(jnp.int32, (256, 256), 0)
    frm = lax.broadcasted_iota(jnp.int32, (256, 256), 1)
    shuffle[...] = (frm == (to % 16) * 16 + to // 16).astype(F32).astype(BF)

    def block_rows(q, z_, c_):
        h = 1 - q // 2
        p = z_ // 2
        s = jnp.where(z_ % 2 == 0, p - q % 2 + 4, p + 1 + q % 2) % 4
        return pl.ds(pl.multiple_of(h * 128 + s * 32 + c_ * 16, 16), 16)

    def pair_copy(kind, q):
        straight = kind == 2 and q == 3
        rows = block_rows(q, mate_z if kind == 2 and not straight else z, c)
        if straight:
            device = at(y, mate_z, 1 - c)
        else:
            device = at(y, mate_z, c) if kind == 0 else at(y, z, 1 - c)
        return pltpu.make_async_remote_copy(
            src_ref=feat.at[rows],
            dst_ref=feat.at[rows],
            send_sem=p2_send.at[kind, q],
            recv_sem=p2_recv.at[kind, q],
            device_id=device,
            device_id_type=MESH,
        )

    def arrived(kind, q):
        rows = block_rows(q, z if kind == 1 else mate_z, c if kind == 0 else 1 - c)
        pltpu.make_async_copy(feat.at[rows], feat.at[rows], p2_recv.at[kind, q]).wait()

    def whiten(h):
        white[h] = lax.dot_general(
            feat[h * 128:(h + 1) * 128], w[...], NT, preferred_element_type=F32
        ).astype(BF)

    me8 = x * NC + c

    def piece(j):
        return pl.ds(pl.multiple_of(j * 16, 16), 16)

    def copy_to(step, k, source, target, device):
        pltpu.make_async_remote_copy(
            src_ref=source,
            dst_ref=target,
            send_sem=rs_send.at[step, k],
            recv_sem=rs_recv.at[step, k],
            device_id=device,
            device_id_type=MESH,
        ).start()

    def await_seven(sems, step, k):
        pltpu.make_async_copy(rs_a.at[0], rs_a.at[0], sems.at[step, k]).wait()

    def scatter(k):
        part[k] = lax.dot_general(white[k], white[1], NT, preferred_element_type=F32)
        for i in (4, 5, 2, 3, 6, 7, 1):
            j = (me8 + i) % 8
            copy_to(0, k, part.at[k, piece(j)], rs_a.at[k, 7 - i], at(y, z, j % NC, j // NC))

    def over_z(k):
        await_seven(rs_recv, 0, k)
        mine[0, k] = part[k, piece(me8)] + jnp.sum(rs_a[k], axis=0)
        for i in (4, 3, 5, 2, 6, 1, 7):
            copy_to(1, k, mine.at[0, k], rs_z.at[k, z], at(y, (z + i) % NZ, c))
        rs_z[k, z] = mine[0, k]

    def over_y(k):
        await_seven(rs_recv, 1, k)
        mine[1, k] = jnp.sum(rs_z[k], axis=0)
        for i in (4, 3, 5, 2, 6, 1, 7):
            copy_to(2, k, mine.at[1, k], rs_y.at[k, y], at((y + i) % NY, z, c))
        rs_y[k, y] = mine[1, k]

    def gather(k):
        await_seven(rs_recv, 2, k)
        full[k, piece(me8)] = jnp.sum(rs_y[k], axis=0)
        for i in (4, 5, 2, 3, 6, 7, 1):
            j = (me8 + i) % 8
            copy_to(3, k, full.at[k, piece(me8)], full.at[k, piece(me8)], at(y, z, j % NC, j // NC))

    for q in range(4):
        h = 1 - q // 2
        block = near_buf.at[h, q % 2]
        pltpu.make_async_copy(block, block, p1_recv.at[h, q % 2]).wait()
        tiles = near_buf[h, q % 2].reshape(256, 128)
        turned = jnp.dot(shuffle[...], tiles, preferred_element_type=F32).astype(BF)
        rows = block_rows(q, z, c)
        for kk in range(16):
            feat[rows, kk * 128:(kk + 1) * 128] = turned[kk * 16:(kk + 1) * 16]
        pair_copy(0, q).start()
        if q == 3:
            pair_copy(2, q).start()
        pair_copy(1, q).start()
        if q > 0:
            arrived(0, q - 1)
            pair_copy(2, q - 1).start()
    for q in range(2):
        arrived(1, q)
        arrived(2, q)
    whiten(1)
    scatter(1)
    for q in range(2, 4):
        if q == 3:
            arrived(0, q)
        arrived(1, q)
        arrived(2, q)
    whiten(0)
    scatter(0)
    over_z(1)
    over_z(0)
    over_y(1)
    over_y(0)
    gather(1)
    gather(0)
    await_seven(rs_recv, 3, 1)
    await_seven(rs_recv, 3, 0)

    count = 32 * NX * 2048
    scores = full[0] * (1.0 / math.sqrt(count))
    gram = full[1] * (1.0 / count)
    level = clip_frac * math.sqrt(128 * 128)

    def times_gram(value):
        return jnp.dot(value, gram, precision=lax.Precision.HIGHEST, preferred_element_type=F32)

    def pace(residual):
        return jnp.minimum(step_rate, level * lax.rsqrt(total(residual * residual) + 1e-06))

    scores_gram = times_gram(scores)
    scores_gram2 = times_gram(scores_gram)
    first = pace(scores)
    now, now_gram = first * scores, first * scores_gram
    residual = scores - now_gram - ridge_shift * now
    residual_gram = scores_gram - first * scores_gram2 - ridge_shift * now_gram
    second = pace(residual)
    now, now_gram = now + second * residual, now_gram + second * residual_gram
    residual = scores - now_gram - ridge_shift * now
    now = now + pace(residual) * residual
    answer[...] = now

    q_y, q_z, q_c, q_e = ex // 32, (ex // 4) % 8, (ex // 2) % 2, ex % 2
    row = ((q_z + 1) // 2) % 4 * 32 + q_c * 16 + q_y * 4 + (q_z + 1) % 2 * 2 + q_e
    line = jnp.broadcast_to(answer[pl.ds(row, 1)], (8, 128))
    t = lax.broadcasted_iota(jnp.int32, (128, 128), 1)
    t_z = (t // 4) % 8
    spot = ((t_z + 1) // 2) % 4 * 32 + (t // 2) % 2 * 16 + t // 32 * 4 + (t_z + 1) % 2 * 2 + t % 2
    pick = (lax.broadcasted_iota(jnp.int32, (128, 128), 0) == spot).astype(F32)
    out_ref[...] = jnp.dot(line, pick, precision=lax.Precision.HIGHEST, preferred_element_type=F32)[:1]

    pltpu.make_async_copy(gbuf.at[:31], gbuf.at[:31], p1_send).wait()
    for kind in range(3):
        for q in range(4):
            pair_copy(kind, q).wait_send()
    for step in range(4):
        for k in range(2):
            await_seven(rs_send, step, k)


def body(activations, output_grads, lengths, whitening):
    hbm = pl.BlockSpec(memory_space=pltpu.HBM)
    return pl.pallas_call(
        kernel,
        out_shape=jax.ShapeDtypeStruct((1, 128), F32),
        in_specs=[hbm, hbm, hbm, hbm],
        out_specs=pl.BlockSpec(memory_space=pltpu.VMEM),
        scratch_shapes=[
            pltpu.SMEM((2,), jnp.int32),
            pltpu.VMEM((2, 32, 64, 128), BF),
            pltpu.VMEM((2, 32, 32, 128), BF),
            pltpu.VMEM((512, 2048), BF),
            pltpu.VMEM((512, 2048), BF),
            pltpu.VMEM((32, 2, 16, 128), BF),
            pltpu.VMEM((2, 2, 8, 2, 16, 128), BF),
            pltpu.VMEM((256, 256), BF),
            pltpu.VMEM((256, 2048), BF),
            pltpu.VMEM((2, 128, 512), BF),
            pltpu.VMEM((2, 128, 128), F32),
            pltpu.VMEM((2, 7, 16, 128), F32),
            pltpu.VMEM((2, 8, 16, 128), F32),
            pltpu.VMEM((2, 8, 16, 128), F32),
            pltpu.VMEM((2, 2, 16, 128), F32),
            pltpu.VMEM((2, 128, 128), F32),
            pltpu.VMEM((128, 128), F32),
            pltpu.SemaphoreType.DMA,
            pltpu.SemaphoreType.DMA((2, 4)),
            pltpu.SemaphoreType.DMA,
            pltpu.SemaphoreType.DMA,
            pltpu.SemaphoreType.DMA((2, 2)),
            pltpu.SemaphoreType.DMA((3, 4)),
            pltpu.SemaphoreType.DMA((3, 4)),
            pltpu.SemaphoreType.DMA((4, 2)),
            pltpu.SemaphoreType.DMA((4, 2)),
        ],
        compiler_params=pltpu.CompilerParams(
            collective_id=0, has_side_effects=True, vmem_limit_bytes=62 * 1024 * 1024
        ),
        cost_estimate=pl.CostEstimate(flops=700_000_000, bytes_accessed=4_000_000, transcendentals=0),
    )(lengths, activations, output_grads, whitening)


def solution(mesh):
    placed = (P("ex", "pp", None, None), P("ex", "pp", None, None), P("ex"), P("ex", "pp", None, None))

    def program(activations, output_grads, lengths, whitening):
        return jax.shard_map(body, mesh=mesh, in_specs=placed, out_specs=P("ex", None), check_vma=False)(
            activations, output_grads, lengths, whitening
        )

    return program
```

```python
import functools
import math

import jax
import jax.numpy as jnp
from jax import lax
from jax.experimental import pallas as pl
from jax.experimental.pallas import tpu as pltpu
from jax.sharding import PartitionSpec as P

MESH = pl.DeviceIdType.MESH
BF = jnp.bfloat16
F32 = jnp.float32
NY, NZ, NC, NX = 8, 8, 2, 4
NT = (((1,), (1,)), ((), ()))

step_rate = 0.5
ridge_shift = 0.5
clip_frac = 0.06


def total(value):
    return jnp.sum(jnp.sum(value, axis=1, keepdims=True), axis=0, keepdims=True)


def kernel(
    len_hbm, act_hbm, grad_hbm, w_hbm, out_ref,
    len_ref,     act, grad, w_in, w, gbuf, near_buf, shuffle, feat, white, part, rs_a, rs_z, rs_y, mine, full, answer,
    len_sem, in_sem, w_sem, p1_send, p1_recv, p2_send, p2_recv, rs_send, rs_recv,
):
    ex = lax.axis_index("ex")
    x = lax.axis_index("pp")
    y = ex // (NZ * NC)
    z = (ex // NC) % NZ
    c = ex % NC
    half = y // 4
    odd = z % 2
    mate_z = z + 1 - 2 * odd

    def at(y_, z_, c_, x_=None):
        return ((y_ * NZ + z_) * NC + c_, x if x_ is None else x_)

    barrier = pltpu.get_barrier_semaphore()
    toward = 2 * odd - 1

    def greet(device):
        pl.semaphore_signal(barrier, inc=1, device_id=device, device_id_type=MESH)

    for dy in (4, 3, 5, 2, 6, 1, 7, 0):
        for d in (3, 2, 1, 0):
            if dy or d:
                greet(at((y + dy) % NY, (z + toward * d + NZ) % NZ, c))
    for i in (4, 3, 5, 2, 6, 1, 7):
        greet(at(y, (z + i) % NZ, c))
    for i in (4, 5, 2, 3, 6, 7, 1):
        greet(at(y, z, (c + i) % 2, (x + i // 2) % NX))
    greet(at(y, mate_z, 1 - c))

    len_copy = pltpu.make_async_copy(len_hbm, len_ref, len_sem)

    def load(j):
        rows = pl.ds(j * 8, 8)
        return (
            pltpu.make_async_copy(act_hbm.at[:, rows], act.at[:, rows], in_sem.at[0, j]),
            pltpu.make_async_copy(grad_hbm.at[:, rows], grad.at[:, rows], in_sem.at[1, j]),
        )

    len_copy.start()
    for j in range(4):
        for copy in load(j):
            copy.start()
    w_copy = pltpu.make_async_copy(w_hbm.at[0, 0], w_in, w_sem)
    w_copy.start()

    lane_low = lax.broadcasted_iota(jnp.int32, (16, 128), 1) < 64
    spots = lax.broadcasted_iota(jnp.int32, (1, 128), 1)
    len_copy.wait()
    masks = [(spots < len_ref[e]).astype(F32).astype(BF) for e in range(2)]

    def gradients(j, _):
        for copy in load(j):
            copy.wait()
        for k in range(8):
            m = j * 8 + k
            for e in range(2):
                a = act[e, m]
                g = grad[e, m] * masks[e]
                twice = jnp.concatenate([a, a], axis=0)
                both = lax.dot_general(g, twice, NT, preferred_element_type=F32)
                gbuf[m, e] = jnp.where(lane_low, both[:16], both[16:]).astype(BF)
        return 0

    lax.fori_loop(0, 4, gradients, 0)

    slot = (y % 4) * 2 + (z + 1) % 2
    pl.semaphore_wait(barrier, 31 + 7 + 7 + 1)
    for far in range(2):
        for dy in (4, 3, 5, 2, 6, 1, 7, 0):
            y_ = (y + dy) % NY
            for k in range(2):
                p = (z // 2 + toward * (2 * far + k) + 4) % 4
                chip = jnp.where((2 * p - z + NZ) % NZ < 4, 2 * p, 2 * p + 1)
                source, target = gbuf.at[y_ * 4 + p], near_buf.at[half, far, slot]
                if dy == 0 and far == 0 and k == 0:
                    pltpu.make_async_copy(source, target, p1_recv.at[half, far]).start()
                else:
                    pltpu.make_async_remote_copy(
                        src_ref=source,
                        dst_ref=target,
                        send_sem=p1_send,
                        recv_sem=p1_recv.at[half, far],
                        device_id=at(y_, chip, c),
                        device_id_type=MESH,
                    ).start()

    w_copy.wait()

    def reorder(r, _):
        rows = pl.ds(r * 32, 32)
        low = lax.broadcasted_iota(jnp.int32, (32, 128), 1) < 64
        for a in range(8):
            t = w_in[rows, a * 128:(a + 1) * 128]
            u = w_in[rows, (8 + a) * 128:(9 + a) * 128]
            t_turned = jnp.concatenate([t[:, 64:], t[:, :64]], axis=1)
            u_turned = jnp.concatenate([u[:, 64:], u[:, :64]], axis=1)
            w[rows, 2 * a * 128:(2 * a + 1) * 128] = jnp.where(low, t, u_turned)
            w[rows, (2 * a + 1) * 128:(2 * a + 2) * 128] = jnp.where(low, t_turned, u)
        return 0

    lax.fori_loop(0, 16, reorder, 0)

    to = lax.broadcasted_iota(jnp.int32, (256, 256), 0)
    frm = lax.broadcasted_iota(jnp.int32, (256, 256), 1)
    shuffle[...] = (frm == (to % 16) * 16 + to // 16).astype(F32).astype(BF)

    def block_rows(q, z_, c_):
        h = 1 - q % 2
        p = z_ // 2
        s = jnp.where(z_ % 2 == 0, p - q // 2 + 4, p + 1 + q // 2) % 4
        return pl.ds(pl.multiple_of(h * 128 + s * 32 + c_ * 16, 16), 16)

    def pair_copy(kind, q):
        straight = kind == 2 and q == 3
        rows = block_rows(q, mate_z if kind == 2 and not straight else z, c)
        if straight:
            device = at(y, mate_z, 1 - c)
        else:
            device = at(y, mate_z, c) if kind == 0 else at(y, z, 1 - c)
        return pltpu.make_async_remote_copy(
            src_ref=feat.at[rows],
            dst_ref=feat.at[rows],
            send_sem=p2_send.at[kind, q],
            recv_sem=p2_recv.at[kind, q],
            device_id=device,
            device_id_type=MESH,
        )

    def arrived(kind, q):
        rows = block_rows(q, z if kind == 1 else mate_z, c if kind == 0 else 1 - c)
        pltpu.make_async_copy(feat.at[rows], feat.at[rows], p2_recv.at[kind, q]).wait()

    def whiten(h):
        white[h] = lax.dot_general(
            feat[h * 128:(h + 1) * 128], w[...], NT, preferred_element_type=F32
        ).astype(BF)

    me8 = x * NC + c

    def piece(j):
        return pl.ds(pl.multiple_of(j * 16, 16), 16)

    def copy_to(step, k, source, target, device):
        pltpu.make_async_remote_copy(
            src_ref=source,
            dst_ref=target,
            send_sem=rs_send.at[step, k],
            recv_sem=rs_recv.at[step, k],
            device_id=device,
            device_id_type=MESH,
        ).start()

    def await_seven(sems, step, k):
        pltpu.make_async_copy(rs_a.at[0], rs_a.at[0], sems.at[step, k]).wait()

    def scatter(k):
        part[k] = lax.dot_general(white[k], white[1], NT, preferred_element_type=F32)
        for i in (4, 5, 2, 3, 6, 7, 1):
            j = (me8 + i) % 8
            copy_to(0, k, part.at[k, piece(j)], rs_a.at[k, 7 - i], at(y, z, j % NC, j // NC))

    def over_z(k):
        await_seven(rs_recv, 0, k)
        mine[0, k] = part[k, piece(me8)] + jnp.sum(rs_a[k], axis=0)
        for i in (4, 3, 5, 2, 6, 1, 7):
            copy_to(1, k, mine.at[0, k], rs_z.at[k, z], at(y, (z + i) % NZ, c))
        rs_z[k, z] = mine[0, k]

    def over_y(k):
        await_seven(rs_recv, 1, k)
        mine[1, k] = jnp.sum(rs_z[k], axis=0)
        for i in (4, 3, 5, 2, 6, 1, 7):
            copy_to(2, k, mine.at[1, k], rs_y.at[k, y], at((y + i) % NY, z, c))
        rs_y[k, y] = mine[1, k]

    def gather(k):
        await_seven(rs_recv, 2, k)
        full[k, piece(me8)] = jnp.sum(rs_y[k], axis=0)
        for i in (4, 5, 2, 3, 6, 7, 1):
            j = (me8 + i) % 8
            copy_to(3, k, full.at[k, piece(me8)], full.at[k, piece(me8)], at(y, z, j % NC, j // NC))

    for q in range(4):
        h, far = 1 - q % 2, q // 2
        block = near_buf.at[h, far]
        pltpu.make_async_copy(block, block, p1_recv.at[h, far]).wait()
        tiles = near_buf[h, far].reshape(256, 128)
        turned = jnp.dot(shuffle[...], tiles, preferred_element_type=F32).astype(BF)
        rows = block_rows(q, z, c)
        for kk in range(16):
            feat[rows, kk * 128:(kk + 1) * 128] = turned[kk * 16:(kk + 1) * 16]
        pair_copy(0, q).start()
        if q == 3:
            pair_copy(2, q).start()
        pair_copy(1, q).start()
    for q in range(3):
        arrived(0, q)
        pair_copy(2, q).start()
    for q in (0, 2):
        arrived(1, q)
        arrived(2, q)
    whiten(1)
    scatter(1)
    for q in (1, 3):
        if q == 3:
            arrived(0, q)
        arrived(1, q)
        arrived(2, q)
    whiten(0)
    scatter(0)
    over_z(1)
    over_z(0)
    over_y(1)
    over_y(0)
    gather(1)
    gather(0)
    await_seven(rs_recv, 3, 1)
    await_seven(rs_recv, 3, 0)

    count = 32 * NX * 2048
    scores = full[0] * (1.0 / math.sqrt(count))
    gram = full[1] * (1.0 / count)
    level = clip_frac * math.sqrt(128 * 128)

    def times_gram(value):
        return jnp.dot(value, gram, precision=lax.Precision.HIGHEST, preferred_element_type=F32)

    def pace(residual):
        return jnp.minimum(step_rate, level * lax.rsqrt(total(residual * residual) + 1e-06))

    scores_gram = times_gram(scores)
    scores_gram2 = times_gram(scores_gram)
    first = pace(scores)
    now, now_gram = first * scores, first * scores_gram
    residual = scores - now_gram - ridge_shift * now
    residual_gram = scores_gram - first * scores_gram2 - ridge_shift * now_gram
    second = pace(residual)
    now, now_gram = now + second * residual, now_gram + second * residual_gram
    residual = scores - now_gram - ridge_shift * now
    now = now + pace(residual) * residual
    answer[...] = now

    q_y, q_z, q_c, q_e = ex // 32, (ex // 4) % 8, (ex // 2) % 2, ex % 2
    row = ((q_z + 1) // 2) % 4 * 32 + q_c * 16 + q_y * 4 + (q_z + 1) % 2 * 2 + q_e
    line = jnp.broadcast_to(answer[pl.ds(row, 1)], (8, 128))
    t = lax.broadcasted_iota(jnp.int32, (128, 128), 1)
    t_z = (t // 4) % 8
    spot = ((t_z + 1) // 2) % 4 * 32 + (t // 2) % 2 * 16 + t // 32 * 4 + (t_z + 1) % 2 * 2 + t % 2
    pick = (lax.broadcasted_iota(jnp.int32, (128, 128), 0) == spot).astype(F32)
    out_ref[...] = jnp.dot(line, pick, precision=lax.Precision.HIGHEST, preferred_element_type=F32)[:1]

    pltpu.make_async_copy(gbuf.at[:31], gbuf.at[:31], p1_send).wait()
    for kind in range(3):
        for q in range(4):
            pair_copy(kind, q).wait_send()
    for step in range(4):
        for k in range(2):
            await_seven(rs_send, step, k)


def body(activations, output_grads, lengths, whitening):
    hbm = pl.BlockSpec(memory_space=pltpu.HBM)
    return pl.pallas_call(
        kernel,
        out_shape=jax.ShapeDtypeStruct((1, 128), F32),
        in_specs=[hbm, hbm, hbm, hbm],
        out_specs=pl.BlockSpec(memory_space=pltpu.VMEM),
        scratch_shapes=[
            pltpu.SMEM((2,), jnp.int32),
            pltpu.VMEM((2, 32, 64, 128), BF),
            pltpu.VMEM((2, 32, 32, 128), BF),
            pltpu.VMEM((512, 2048), BF),
            pltpu.VMEM((512, 2048), BF),
            pltpu.VMEM((32, 2, 16, 128), BF),
            pltpu.VMEM((2, 2, 8, 2, 16, 128), BF),
            pltpu.VMEM((256, 256), BF),
            pltpu.VMEM((256, 2048), BF),
            pltpu.VMEM((2, 128, 512), BF),
            pltpu.VMEM((2, 128, 128), F32),
            pltpu.VMEM((2, 7, 16, 128), F32),
            pltpu.VMEM((2, 8, 16, 128), F32),
            pltpu.VMEM((2, 8, 16, 128), F32),
            pltpu.VMEM((2, 2, 16, 128), F32),
            pltpu.VMEM((2, 128, 128), F32),
            pltpu.VMEM((128, 128), F32),
            pltpu.SemaphoreType.DMA,
            pltpu.SemaphoreType.DMA((2, 4)),
            pltpu.SemaphoreType.DMA,
            pltpu.SemaphoreType.DMA,
            pltpu.SemaphoreType.DMA((2, 2)),
            pltpu.SemaphoreType.DMA((3, 4)),
            pltpu.SemaphoreType.DMA((3, 4)),
            pltpu.SemaphoreType.DMA((4, 2)),
            pltpu.SemaphoreType.DMA((4, 2)),
        ],
        compiler_params=pltpu.CompilerParams(
            collective_id=0, has_side_effects=True, vmem_limit_bytes=62 * 1024 * 1024
        ),
        cost_estimate=pl.CostEstimate(flops=700_000_000, bytes_accessed=4_000_000, transcendentals=0),
    )(lengths, activations, output_grads, whitening)


def solution(mesh):
    placed = (P("ex", "pp", None, None), P("ex", "pp", None, None), P("ex"), P("ex", "pp", None, None))

    def program(activations, output_grads, lengths, whitening):
        return jax.shard_map(body, mesh=mesh, in_specs=placed, out_specs=P("ex", None), check_vma=False)(
            activations, output_grads, lengths, whitening
        )

    return program
```

```python
import functools
import math

import jax
import jax.numpy as jnp
from jax import lax
from jax.experimental import pallas as pl
from jax.experimental.pallas import tpu as pltpu
from jax.sharding import PartitionSpec as P

MESH = pl.DeviceIdType.MESH
BF = jnp.bfloat16
F32 = jnp.float32
NY, NZ, NC, NX = 8, 8, 2, 4
NT = (((1,), (1,)), ((), ()))

step_rate = 0.5
ridge_shift = 0.5
clip_frac = 0.06


def total(value):
    return jnp.sum(jnp.sum(value, axis=1, keepdims=True), axis=0, keepdims=True)


def kernel(
    len_hbm, act_hbm, grad_hbm, w_hbm, out_ref,
    len_ref,     act, grad, w_in, w, gbuf, near_buf, shuffle, feat, white, part, rs_a, rs_z, rs_y, mine, full, answer,
    len_sem, in_sem, w_sem, p1_send, p1_recv, p2_send, p2_recv, rs_send, rs_recv,
):
    ex = lax.axis_index("ex")
    x = lax.axis_index("pp")
    y = ex // (NZ * NC)
    z = (ex // NC) % NZ
    c = ex % NC
    half = y // 4
    odd = z % 2
    mate_z = z + 1 - 2 * odd

    def at(y_, z_, c_, x_=None):
        return ((y_ * NZ + z_) * NC + c_, x if x_ is None else x_)

    barrier = pltpu.get_barrier_semaphore()
    toward = 2 * odd - 1

    def greet(device):
        pl.semaphore_signal(barrier, inc=1, device_id=device, device_id_type=MESH)

    far_first = sorted(
        [(dy, d) for dy in range(NY) for d in range(4) if dy or d], key=lambda v: -min(v[0], NY - v[0]) - v[1]
    )
    for dy, d in far_first:
        greet(at((y + dy) % NY, (z + toward * d + NZ) % NZ, c))
    for i in (4, 3, 5, 2, 6, 1, 7):
        greet(at(y, (z + i) % NZ, c))
    for i in (4, 5, 2, 3, 6, 7, 1):
        greet(at(y, z, (c + i) % 2, (x + i // 2) % NX))
    greet(at(y, mate_z, 1 - c))

    len_copy = pltpu.make_async_copy(len_hbm, len_ref, len_sem)

    def load(j):
        rows = pl.ds(j * 8, 8)
        return (
            pltpu.make_async_copy(act_hbm.at[:, rows], act.at[:, rows], in_sem.at[0, j]),
            pltpu.make_async_copy(grad_hbm.at[:, rows], grad.at[:, rows], in_sem.at[1, j]),
        )

    len_copy.start()
    for j in range(4):
        for copy in load(j):
            copy.start()
    w_copy = pltpu.make_async_copy(w_hbm.at[0, 0], w_in, w_sem)
    w_copy.start()

    lane_low = lax.broadcasted_iota(jnp.int32, (16, 128), 1) < 64
    spots = lax.broadcasted_iota(jnp.int32, (1, 128), 1)
    len_copy.wait()
    masks = [(spots < len_ref[e]).astype(F32).astype(BF) for e in range(2)]

    def gradients(j, _):
        for copy in load(j):
            copy.wait()
        for k in range(8):
            m = j * 8 + k
            for e in range(2):
                a = act[e, m]
                g = grad[e, m] * masks[e]
                twice = jnp.concatenate([a, a], axis=0)
                both = lax.dot_general(g, twice, NT, preferred_element_type=F32)
                gbuf[m, e] = jnp.where(lane_low, both[:16], both[16:]).astype(BF)
        return 0

    lax.fori_loop(0, 4, gradients, 0)

    slot = (y % 4) * 2 + (z + 1) % 2
    pl.semaphore_wait(barrier, 31 + 7 + 7 + 1)
    for far in range(2):
        for dy in (4, 3, 5, 2, 6, 1, 7, 0):
            y_ = (y + dy) % NY
            for k in range(2):
                p = (z // 2 + toward * (2 * far + k) + 4) % 4
                chip = jnp.where((2 * p - z + NZ) % NZ < 4, 2 * p, 2 * p + 1)
                source, target = gbuf.at[y_ * 4 + p], near_buf.at[half, far, slot]
                if dy == 0 and far == 0 and k == 0:
                    pltpu.make_async_copy(source, target, p1_recv.at[half, far]).start()
                else:
                    pltpu.make_async_remote_copy(
                        src_ref=source,
                        dst_ref=target,
                        send_sem=p1_send,
                        recv_sem=p1_recv.at[half, far],
                        device_id=at(y_, chip, c),
                        device_id_type=MESH,
                    ).start()

    w_copy.wait()

    def reorder(r, _):
        rows = pl.ds(r * 32, 32)
        low = lax.broadcasted_iota(jnp.int32, (32, 128), 1) < 64
        for a in range(8):
            t = w_in[rows, a * 128:(a + 1) * 128]
            u = w_in[rows, (8 + a) * 128:(9 + a) * 128]
            t_turned = jnp.concatenate([t[:, 64:], t[:, :64]], axis=1)
            u_turned = jnp.concatenate([u[:, 64:], u[:, :64]], axis=1)
            w[rows, 2 * a * 128:(2 * a + 1) * 128] = jnp.where(low, t, u_turned)
            w[rows, (2 * a + 1) * 128:(2 * a + 2) * 128] = jnp.where(low, t_turned, u)
        return 0

    lax.fori_loop(0, 16, reorder, 0)

    to = lax.broadcasted_iota(jnp.int32, (256, 256), 0)
    frm = lax.broadcasted_iota(jnp.int32, (256, 256), 1)
    shuffle[...] = (frm == (to % 16) * 16 + to // 16).astype(F32).astype(BF)

    def block_rows(q, z_, c_):
        h = 1 - q % 2
        p = z_ // 2
        s = jnp.where(z_ % 2 == 0, p - q // 2 + 4, p + 1 + q // 2) % 4
        return pl.ds(pl.multiple_of(h * 128 + s * 32 + c_ * 16, 16), 16)

    def pair_copy(kind, q):
        straight = kind == 2 and q == 3
        rows = block_rows(q, mate_z if kind == 2 and not straight else z, c)
        if straight:
            device = at(y, mate_z, 1 - c)
        else:
            device = at(y, mate_z, c) if kind == 0 else at(y, z, 1 - c)
        return pltpu.make_async_remote_copy(
            src_ref=feat.at[rows],
            dst_ref=feat.at[rows],
            send_sem=p2_send.at[kind, q],
            recv_sem=p2_recv.at[kind, q],
            device_id=device,
            device_id_type=MESH,
        )

    def arrived(kind, q):
        rows = block_rows(q, z if kind == 1 else mate_z, c if kind == 0 else 1 - c)
        pltpu.make_async_copy(feat.at[rows], feat.at[rows], p2_recv.at[kind, q]).wait()

    def whiten(h):
        white[h] = lax.dot_general(
            feat[h * 128:(h + 1) * 128], w[...], NT, preferred_element_type=F32
        ).astype(BF)

    me8 = x * NC + c

    def piece(j):
        return pl.ds(pl.multiple_of(j * 16, 16), 16)

    def copy_to(step, k, source, target, device):
        pltpu.make_async_remote_copy(
            src_ref=source,
            dst_ref=target,
            send_sem=rs_send.at[step, k],
            recv_sem=rs_recv.at[step, k],
            device_id=device,
            device_id_type=MESH,
        ).start()

    def await_seven(sems, step, k):
        pltpu.make_async_copy(rs_a[k], rs_a[k], sems.at[step, k]).wait()

    def sum_of(stack):
        return jnp.sum(stack[...].astype(F32), axis=0)

    def scatter(k):
        part[k][...] = lax.dot_general(white[k], white[1], NT, preferred_element_type=F32).astype(part[k].dtype)
        for i in (4, 5, 2, 3, 6, 7, 1):
            j = (me8 + i) % 8
            copy_to(0, k, part[k].at[piece(j)], rs_a[k].at[7 - i], at(y, z, j % NC, j // NC))

    def over_z(k):
        await_seven(rs_recv, 0, k)
        mine[k][0] = (part[k][piece(me8)].astype(F32) + sum_of(rs_a[k])).astype(part[k].dtype)
        for i in (4, 3, 5, 2, 6, 1, 7):
            copy_to(1, k, mine[k].at[0], rs_z[k].at[z], at(y, (z + i) % NZ, c))
        rs_z[k][z] = mine[k][0]

    def over_y(k):
        await_seven(rs_recv, 1, k)
        mine[k][1] = sum_of(rs_z[k]).astype(part[k].dtype)
        for i in (4, 3, 5, 2, 6, 1, 7):
            copy_to(2, k, mine[k].at[1], rs_y[k].at[y], at((y + i) % NY, z, c))
        rs_y[k][y] = mine[k][1]

    def gather(k):
        await_seven(rs_recv, 2, k)
        own = full[k].at[piece(me8)]
        own[...] = sum_of(rs_y[k]).astype(part[k].dtype)
        for i in (4, 5, 2, 3, 6, 7, 1):
            j = (me8 + i) % 8
            copy_to(3, k, own, own, at(y, z, j % NC, j // NC))

    for q in range(4):
        h, far = 1 - q % 2, q // 2
        block = near_buf.at[h, far]
        pltpu.make_async_copy(block, block, p1_recv.at[h, far]).wait()
        tiles = near_buf[h, far].reshape(256, 128)
        turned = jnp.dot(shuffle[...], tiles, preferred_element_type=F32).astype(BF)
        rows = block_rows(q, z, c)
        for kk in range(16):
            feat[rows, kk * 128:(kk + 1) * 128] = turned[kk * 16:(kk + 1) * 16]
        pair_copy(0, q).start()
        if q == 3:
            pair_copy(2, q).start()
        pair_copy(1, q).start()
    for q in range(3):
        arrived(0, q)
        pair_copy(2, q).start()
    for q in (0, 2):
        arrived(1, q)
        arrived(2, q)
    whiten(1)
    scatter(1)
    for q in (1, 3):
        if q == 3:
            arrived(0, q)
        arrived(1, q)
        arrived(2, q)
    whiten(0)
    scatter(0)
    over_z(1)
    over_z(0)
    over_y(1)
    over_y(0)
    gather(1)
    gather(0)
    await_seven(rs_recv, 3, 1)
    await_seven(rs_recv, 3, 0)

    count = 32 * NX * 2048
    scores = full[0][...] * (1.0 / math.sqrt(count))
    gram = full[1][...] * BF(1.0 / count)
    level = clip_frac * math.sqrt(128 * 128)

    def times_gram(value):
        high = value.astype(BF)
        rest = value - high.astype(F32)
        middle = rest.astype(BF)
        low = (rest - middle.astype(F32)).astype(BF)
        product = jnp.dot(jnp.concatenate([high, middle, low], axis=0), gram, preferred_element_type=F32)
        return product[:128] + product[128:256] + product[256:]

    def pace(residual):
        return jnp.minimum(step_rate, level * lax.rsqrt(total(residual * residual) + 1e-06))

    scores_gram = times_gram(scores)
    scores_gram2 = times_gram(scores_gram)
    first = pace(scores)
    now, now_gram = first * scores, first * scores_gram
    residual = scores - now_gram - ridge_shift * now
    residual_gram = scores_gram - first * scores_gram2 - ridge_shift * now_gram
    second = pace(residual)
    now, now_gram = now + second * residual, now_gram + second * residual_gram
    residual = scores - now_gram - ridge_shift * now
    answer[0], answer[1] = now, residual

    q_y, q_z, q_c, q_e = ex // 32, (ex // 4) % 8, (ex // 2) % 2, ex % 2
    row = ((q_z + 1) // 2) % 4 * 32 + q_c * 16 + q_y * 4 + (q_z + 1) % 2 * 2 + q_e
    top = lax.broadcasted_iota(jnp.int32, (8, 128), 0) == 0
    lines = jnp.where(
        top,
        jnp.broadcast_to(answer[0, pl.ds(row, 1)], (8, 128)),
        jnp.broadcast_to(answer[1, pl.ds(row, 1)], (8, 128)),
    )
    t = lax.broadcasted_iota(jnp.int32, (128, 128), 1)
    t_z = (t // 4) % 8
    spot = ((t_z + 1) // 2) % 4 * 32 + (t // 2) % 2 * 16 + t // 32 * 4 + (t_z + 1) % 2 * 2 + t % 2
    pick = (lax.broadcasted_iota(jnp.int32, (128, 128), 0) == spot).astype(F32)
    ordered = jnp.dot(lines, pick, precision=lax.Precision.HIGHEST, preferred_element_type=F32)
    out_ref[...] = ordered[:1] + pace(residual) * ordered[1:2]

    pltpu.make_async_copy(gbuf.at[:31], gbuf.at[:31], p1_send).wait()
    for kind in range(3):
        for q in range(4):
            pair_copy(kind, q).wait_send()
    for step in range(4):
        for k in range(2):
            await_seven(rs_send, step, k)


def body(activations, output_grads, lengths, whitening):
    hbm = pl.BlockSpec(memory_space=pltpu.HBM)
    return pl.pallas_call(
        kernel,
        out_shape=jax.ShapeDtypeStruct((1, 128), F32),
        in_specs=[hbm, hbm, hbm, hbm],
        out_specs=pl.BlockSpec(memory_space=pltpu.VMEM),
        scratch_shapes=[
            pltpu.SMEM((2,), jnp.int32),
            pltpu.VMEM((2, 32, 64, 128), BF),
            pltpu.VMEM((2, 32, 32, 128), BF),
            pltpu.VMEM((512, 2048), BF),
            pltpu.VMEM((512, 2048), BF),
            pltpu.VMEM((32, 2, 16, 128), BF),
            pltpu.VMEM((2, 2, 8, 2, 16, 128), BF),
            pltpu.VMEM((256, 256), BF),
            pltpu.VMEM((256, 2048), BF),
            pltpu.VMEM((2, 128, 512), BF),
            [pltpu.VMEM((128, 128), dtype) for dtype in (F32, BF)],
            [pltpu.VMEM((7, 16, 128), dtype) for dtype in (F32, BF)],
            [pltpu.VMEM((8, 16, 128), dtype) for dtype in (F32, BF)],
            [pltpu.VMEM((8, 16, 128), dtype) for dtype in (F32, BF)],
            [pltpu.VMEM((2, 16, 128), dtype) for dtype in (F32, BF)],
            [pltpu.VMEM((128, 128), dtype) for dtype in (F32, BF)],
            pltpu.VMEM((2, 128, 128), F32),
            pltpu.SemaphoreType.DMA,
            pltpu.SemaphoreType.DMA((2, 4)),
            pltpu.SemaphoreType.DMA,
            pltpu.SemaphoreType.DMA,
            pltpu.SemaphoreType.DMA((2, 2)),
            pltpu.SemaphoreType.DMA((3, 4)),
            pltpu.SemaphoreType.DMA((3, 4)),
            pltpu.SemaphoreType.DMA((4, 2)),
            pltpu.SemaphoreType.DMA((4, 2)),
        ],
        compiler_params=pltpu.CompilerParams(
            collective_id=0, has_side_effects=True, vmem_limit_bytes=62 * 1024 * 1024
        ),
        cost_estimate=pl.CostEstimate(flops=700_000_000, bytes_accessed=4_000_000, transcendentals=0),
    )(lengths, activations, output_grads, whitening)


def solution(mesh):
    placed = (P("ex", "pp", None, None), P("ex", "pp", None, None), P("ex"), P("ex", "pp", None, None))

    def program(activations, output_grads, lengths, whitening):
        return jax.shard_map(body, mesh=mesh, in_specs=placed, out_specs=P("ex", None), check_vma=False)(
            activations, output_grads, lengths, whitening
        )

    return program
```

```python
import functools
import math

import jax
import jax.numpy as jnp
from jax import lax
from jax.experimental import pallas as pl
from jax.experimental.pallas import tpu as pltpu
from jax.sharding import PartitionSpec as P

MESH = pl.DeviceIdType.MESH
BF = jnp.bfloat16
F32 = jnp.float32
NY, NZ, NC, NX = 8, 8, 2, 4
NT = (((1,), (1,)), ((), ()))

step_rate = 0.5
ridge_shift = 0.5
clip_frac = 0.06


def total(value):
    return jnp.sum(jnp.sum(value, axis=1, keepdims=True), axis=0, keepdims=True)


def mod(value, size):
    return lax.rem(value, jnp.int32(size))


def div(value, size):
    return lax.div(value, jnp.int32(size))


def kernel(
    len_hbm, act_hbm, grad_hbm, w_hbm, out_ref,
    len_ref,     act, grad, w_in, w, gbuf, near_buf, shuffle, feat, white, part, rs_a, rs_z, rs_y, mine, full, answer,
    len_sem, in_sem, w_sem, p1_send, p1_recv, p2_send, p2_recv, rs_send, rs_recv,
):
    ex = lax.axis_index("ex")
    x = lax.axis_index("pp")
    y = div(ex, NZ * NC)
    z = mod(div(ex, NC), NZ)
    c = mod(ex, NC)
    half = div(y, 4)
    odd = mod(z, 2)
    mate_z = z + 1 - 2 * odd

    def at(y_, z_, c_, x_=None):
        return ((y_ * NZ + z_) * NC + c_, x if x_ is None else x_)

    barrier = pltpu.get_barrier_semaphore()
    toward = 2 * odd - 1

    def greet(device):
        pl.semaphore_signal(barrier, inc=1, device_id=device, device_id_type=MESH)

    far_first = sorted(
        [(dy, d) for dy in range(NY) for d in range(4) if dy or d], key=lambda v: -min(v[0], NY - v[0]) - v[1]
    )
    for dy, d in far_first:
        greet(at(mod(y + dy, NY), mod(z + toward * d + NZ, NZ), c))
    for i in (4, 3, 5, 2, 6, 1, 7):
        greet(at(y, mod(z + i, NZ), c))
    for i in (4, 5, 2, 3, 6, 7, 1):
        greet(at(y, z, mod(c + i, 2), mod(x + i // 2, NX)))
    greet(at(y, mate_z, 1 - c))

    len_copy = pltpu.make_async_copy(len_hbm, len_ref, len_sem)

    def load(j):
        rows = pl.ds(j * 8, 8)
        return (
            pltpu.make_async_copy(act_hbm.at[:, rows], act.at[:, rows], in_sem.at[0, j]),
            pltpu.make_async_copy(grad_hbm.at[:, rows], grad.at[:, rows], in_sem.at[1, j]),
        )

    len_copy.start()
    for j in range(4):
        for copy in load(j):
            copy.start()
    w_copy = pltpu.make_async_copy(w_hbm.at[0, 0], w_in, w_sem)
    w_copy.start()

    lane_low = lax.broadcasted_iota(jnp.int32, (16, 128), 1) < 64
    spots = lax.broadcasted_iota(jnp.int32, (1, 128), 1)
    len_copy.wait()
    masks = [(spots < len_ref[e]).astype(F32).astype(BF) for e in range(2)]

    def gradients(j, _):
        for copy in load(j):
            copy.wait()
        for k in range(8):
            m = j * 8 + k
            for e in range(2):
                a = act[e, m]
                g = grad[e, m] * masks[e]
                twice = jnp.concatenate([a, a], axis=0)
                both = lax.dot_general(g, twice, NT, preferred_element_type=F32)
                gbuf[m, e] = jnp.where(lane_low, both[:16], both[16:]).astype(BF)
        return 0

    lax.fori_loop(0, 4, gradients, 0)

    slot = (y % 4) * 2 + (z + 1) % 2
    pl.semaphore_wait(barrier, 31 + 7 + 7 + 1)
    for far in range(2):
        for dy in (4, 3, 5, 2, 6, 1, 7, 0):
            y_ = mod(y + dy, NY)
            for k in range(2):
                p = mod(div(z, 2) + toward * (2 * far + k) + 4, 4)
                chip = jnp.where(mod(2 * p - z + NZ, NZ) < 4, 2 * p, 2 * p + 1)
                source, target = gbuf.at[y_ * 4 + p], near_buf.at[half, far, slot]
                if dy == 0 and far == 0 and k == 0:
                    pltpu.make_async_copy(source, target, p1_recv.at[half, far]).start()
                else:
                    pltpu.make_async_remote_copy(
                        src_ref=source,
                        dst_ref=target,
                        send_sem=p1_send,
                        recv_sem=p1_recv.at[half, far],
                        device_id=at(y_, chip, c),
                        device_id_type=MESH,
                    ).start()

    w_copy.wait()

    def reorder(r, _):
        rows = pl.ds(r * 32, 32)
        low = lax.broadcasted_iota(jnp.int32, (32, 128), 1) < 64
        for a in range(8):
            t = w_in[rows, a * 128:(a + 1) * 128]
            u = w_in[rows, (8 + a) * 128:(9 + a) * 128]
            t_turned = jnp.concatenate([t[:, 64:], t[:, :64]], axis=1)
            u_turned = jnp.concatenate([u[:, 64:], u[:, :64]], axis=1)
            w[rows, 2 * a * 128:(2 * a + 1) * 128] = jnp.where(low, t, u_turned)
            w[rows, (2 * a + 1) * 128:(2 * a + 2) * 128] = jnp.where(low, t_turned, u)
        return 0

    lax.fori_loop(0, 16, reorder, 0)

    to = lax.broadcasted_iota(jnp.int32, (256, 256), 0)
    frm = lax.broadcasted_iota(jnp.int32, (256, 256), 1)
    shuffle[...] = (frm == (to % 16) * 16 + to // 16).astype(F32).astype(BF)

    def block_rows(q, z_, c_):
        h = 1 - q % 2
        p = z_ // 2
        s = jnp.where(z_ % 2 == 0, p - q // 2 + 4, p + 1 + q // 2) % 4
        return pl.ds(pl.multiple_of(h * 128 + s * 32 + c_ * 16, 16), 16)

    def pair_copy(kind, q):
        straight = kind == 2 and q == 3
        rows = block_rows(q, mate_z if kind == 2 and not straight else z, c)
        if straight:
            device = at(y, mate_z, 1 - c)
        else:
            device = at(y, mate_z, c) if kind == 0 else at(y, z, 1 - c)
        return pltpu.make_async_remote_copy(
            src_ref=feat.at[rows],
            dst_ref=feat.at[rows],
            send_sem=p2_send.at[kind, q],
            recv_sem=p2_recv.at[kind, q],
            device_id=device,
            device_id_type=MESH,
        )

    def arrived(kind, q):
        rows = block_rows(q, z if kind == 1 else mate_z, c if kind == 0 else 1 - c)
        pltpu.make_async_copy(feat.at[rows], feat.at[rows], p2_recv.at[kind, q]).wait()

    def whiten(h):
        white[h] = lax.dot_general(
            feat[h * 128:(h + 1) * 128], w[...], NT, preferred_element_type=F32
        ).astype(BF)

    me8 = x * NC + c

    def piece(j):
        return pl.ds(pl.multiple_of(j * 16, 16), 16)

    def copy_to(step, k, source, target, device):
        pltpu.make_async_remote_copy(
            src_ref=source,
            dst_ref=target,
            send_sem=rs_send.at[step, k],
            recv_sem=rs_recv.at[step, k],
            device_id=device,
            device_id_type=MESH,
        ).start()

    def await_seven(sems, step, k):
        pltpu.make_async_copy(rs_a[k], rs_a[k], sems.at[step, k]).wait()

    def sum_of(stack):
        return jnp.sum(stack[...].astype(F32), axis=0)

    def scatter(k):
        part[k][...] = lax.dot_general(white[k], white[1], NT, preferred_element_type=F32).astype(part[k].dtype)
        for i in (4, 5, 2, 3, 6, 7, 1):
            j = mod(me8 + i, 8)
            copy_to(0, k, part[k].at[piece(j)], rs_a[k].at[7 - i], at(y, z, mod(j, NC), div(j, NC)))

    def over_z(k):
        await_seven(rs_recv, 0, k)
        mine[k][0] = (part[k][piece(me8)].astype(F32) + sum_of(rs_a[k])).astype(part[k].dtype)
        for i in (4, 3, 5, 2, 6, 1, 7):
            copy_to(1, k, mine[k].at[0], rs_z[k].at[z], at(y, mod(z + i, NZ), c))
        rs_z[k][z] = mine[k][0]

    def over_y(k):
        await_seven(rs_recv, 1, k)
        mine[k][1] = sum_of(rs_z[k]).astype(part[k].dtype)
        for i in (4, 3, 5, 2, 6, 1, 7):
            copy_to(2, k, mine[k].at[1], rs_y[k].at[y], at(mod(y + i, NY), z, c))
        rs_y[k][y] = mine[k][1]

    def gather(k):
        await_seven(rs_recv, 2, k)
        own = full[k].at[piece(me8)]
        own[...] = sum_of(rs_y[k]).astype(part[k].dtype)
        for i in (4, 5, 2, 3, 6, 7, 1):
            j = mod(me8 + i, 8)
            copy_to(3, k, own, own, at(y, z, mod(j, NC), div(j, NC)))

    for q in range(4):
        h, far = 1 - q % 2, q // 2
        block = near_buf.at[h, far]
        pltpu.make_async_copy(block, block, p1_recv.at[h, far]).wait()
        tiles = near_buf[h, far].reshape(256, 128)
        turned = jnp.dot(shuffle[...], tiles, preferred_element_type=F32).astype(BF)
        rows = block_rows(q, z, c)
        for kk in range(16):
            feat[rows, kk * 128:(kk + 1) * 128] = turned[kk * 16:(kk + 1) * 16]
        pair_copy(0, q).start()
        if q == 3:
            pair_copy(2, q).start()
        pair_copy(1, q).start()
    for q in range(3):
        arrived(0, q)
        pair_copy(2, q).start()
    for q in (0, 2):
        arrived(1, q)
        arrived(2, q)
    whiten(1)
    scatter(1)
    for q in (1, 3):
        if q == 3:
            arrived(0, q)
        arrived(1, q)
        arrived(2, q)
    whiten(0)
    scatter(0)
    over_z(1)
    over_z(0)
    over_y(1)
    over_y(0)
    gather(1)
    gather(0)
    await_seven(rs_recv, 3, 1)
    await_seven(rs_recv, 3, 0)

    count = 32 * NX * 2048
    scores = full[0][...] * (1.0 / math.sqrt(count))
    gram = full[1][...] * BF(1.0 / count)
    level = clip_frac * math.sqrt(128 * 128)

    def times_gram(value):
        high = value.astype(BF)
        rest = value - high.astype(F32)
        middle = rest.astype(BF)
        low = (rest - middle.astype(F32)).astype(BF)
        product = jnp.dot(jnp.concatenate([high, middle, low], axis=0), gram, preferred_element_type=F32)
        return product[:128] + product[128:256] + product[256:]

    def pace(residual):
        return jnp.minimum(step_rate, level * lax.rsqrt(total(residual * residual) + 1e-06))

    scores_gram = times_gram(scores)
    scores_gram2 = times_gram(scores_gram)
    first = pace(scores)
    now, now_gram = first * scores, first * scores_gram
    residual = scores - now_gram - ridge_shift * now
    residual_gram = scores_gram - first * scores_gram2 - ridge_shift * now_gram
    second = pace(residual)
    now, now_gram = now + second * residual, now_gram + second * residual_gram
    residual = scores - now_gram - ridge_shift * now
    answer[0], answer[1] = now, residual

    q_y, q_z, q_c, q_e = ex // 32, (ex // 4) % 8, (ex // 2) % 2, ex % 2
    row = ((q_z + 1) // 2) % 4 * 32 + q_c * 16 + q_y * 4 + (q_z + 1) % 2 * 2 + q_e
    top = lax.broadcasted_iota(jnp.int32, (8, 128), 0) == 0
    lines = jnp.where(
        top,
        jnp.broadcast_to(answer[0, pl.ds(row, 1)], (8, 128)),
        jnp.broadcast_to(answer[1, pl.ds(row, 1)], (8, 128)),
    )
    t = lax.broadcasted_iota(jnp.int32, (128, 128), 1)
    t_z = (t // 4) % 8
    spot = ((t_z + 1) // 2) % 4 * 32 + (t // 2) % 2 * 16 + t // 32 * 4 + (t_z + 1) % 2 * 2 + t % 2
    pick = (lax.broadcasted_iota(jnp.int32, (128, 128), 0) == spot).astype(F32)
    ordered = jnp.dot(lines, pick, precision=lax.Precision.HIGHEST, preferred_element_type=F32)
    out_ref[...] = ordered[:1] + pace(residual) * ordered[1:2]

    pltpu.make_async_copy(gbuf.at[:31], gbuf.at[:31], p1_send).wait()
    for kind in range(3):
        for q in range(4):
            pair_copy(kind, q).wait_send()
    for step in range(4):
        for k in range(2):
            await_seven(rs_send, step, k)


def body(activations, output_grads, lengths, whitening):
    hbm = pl.BlockSpec(memory_space=pltpu.HBM)
    return pl.pallas_call(
        kernel,
        out_shape=jax.ShapeDtypeStruct((1, 128), F32),
        in_specs=[hbm, hbm, hbm, hbm],
        out_specs=pl.BlockSpec(memory_space=pltpu.VMEM),
        scratch_shapes=[
            pltpu.SMEM((2,), jnp.int32),
            pltpu.VMEM((2, 32, 64, 128), BF),
            pltpu.VMEM((2, 32, 32, 128), BF),
            pltpu.VMEM((512, 2048), BF),
            pltpu.VMEM((512, 2048), BF),
            pltpu.VMEM((32, 2, 16, 128), BF),
            pltpu.VMEM((2, 2, 8, 2, 16, 128), BF),
            pltpu.VMEM((256, 256), BF),
            pltpu.VMEM((256, 2048), BF),
            pltpu.VMEM((2, 128, 512), BF),
            [pltpu.VMEM((128, 128), dtype) for dtype in (F32, BF)],
            [pltpu.VMEM((7, 16, 128), dtype) for dtype in (F32, BF)],
            [pltpu.VMEM((8, 16, 128), dtype) for dtype in (F32, BF)],
            [pltpu.VMEM((8, 16, 128), dtype) for dtype in (F32, BF)],
            [pltpu.VMEM((2, 16, 128), dtype) for dtype in (F32, BF)],
            [pltpu.VMEM((128, 128), dtype) for dtype in (F32, BF)],
            pltpu.VMEM((2, 128, 128), F32),
            pltpu.SemaphoreType.DMA,
            pltpu.SemaphoreType.DMA((2, 4)),
            pltpu.SemaphoreType.DMA,
            pltpu.SemaphoreType.DMA,
            pltpu.SemaphoreType.DMA((2, 2)),
            pltpu.SemaphoreType.DMA((3, 4)),
            pltpu.SemaphoreType.DMA((3, 4)),
            pltpu.SemaphoreType.DMA((4, 2)),
            pltpu.SemaphoreType.DMA((4, 2)),
        ],
        compiler_params=pltpu.CompilerParams(
            collective_id=0, has_side_effects=True, vmem_limit_bytes=62 * 1024 * 1024
        ),
        cost_estimate=pl.CostEstimate(flops=700_000_000, bytes_accessed=4_000_000, transcendentals=0),
    )(lengths, activations, output_grads, whitening)


def solution(mesh):
    placed = (P("ex", "pp", None, None), P("ex", "pp", None, None), P("ex"), P("ex", "pp", None, None))

    def program(activations, output_grads, lengths, whitening):
        return jax.shard_map(body, mesh=mesh, in_specs=placed, out_specs=P("ex", None), check_vma=False)(
            activations, output_grads, lengths, whitening
        )

    return program
```
